32 devices in a mesh: groups: 2 (over x), query: 16 (over z, y, core).
Axes of the slice: x: 2, y: 2, z: 4, core: 2. Of those that a mesh axis runs over, the one named last changes fastest.
Arguments:
- tokens: bfloat16 [384, 4096], P(('groups', 'query')), parts along dimension 0, may hold values from -6 to 6
- grad_out: bfloat16 [384, 4096], P(('groups', 'query')), parts along dimension 0, may hold values from -6 to 6
- gate_weight: bfloat16 [4096, 14336], P(None, 'query'), may hold values from -0.09375 to 0.09375
- up_weight: bfloat16 [4096, 14336], P(None, 'query'), may hold values from -0.09375 to 0.09375
- query_left: bfloat16 [16, 4096, 32], P('query'), may hold values from -0.09375 to 0.09375
- query_right: bfloat16 [16, 14336, 32], P('query'), may hold values from -0.09375 to 0.09375
Outputs:
- scores: float32 [384, 16], P(('groups', 'query')), parts along dimension 0
The draws below stay inside these ranges and needn't reach their ends.
There are 2 independent parts, one for each index of `groups`. The reference program is written for one: setup_inputs(seed, part) draws one part's arguments, and reference() takes and returns one part's arrays. A program takes and returns all parts, laid end to end along the dimension named above; an argument that names none is the same for every part. Nothing has to cross between parts.
All inputs are finite; a program needn't handle non-finite values.
Results may differ from the reference program's by a relative error of at most 0.0003.
Values may be sent and summed in bfloat16 or wider, within the bound.
No kernel may reach another device: no remote copies, remote signals or barrier semaphores. Data moves between devices by JAX's collectives and lax.ppermute only.
A program may use at most 128 MiB of HBM per device.

```python
import jax
import jax.numpy as jnp
from jax import lax

D = 4096
FF = 14336
RANK = 32
TOKENS = 192
QUERIES = 16


def levels(stream_key, extent, shards, low, largest):
    loudness = 1.0
    for axis_at, shards_of in shards:
        heights = jax.random.uniform(jax.random.fold_in(jax.random.fold_in(stream_key, 6), axis_at), (shards_of,), jnp.float32, low / len(shards), largest / len(shards))
        loudness = loudness * jnp.repeat(jnp.exp(heights), extent[axis_at] // shards_of).reshape((-1,) + (1,) * (len(extent) - 1 - axis_at))
    return loudness


def gaussian(key, dims, scale, reach, pieces=(), held_as=jnp.bfloat16):
    values = scale * jax.random.normal(key, dims, jnp.float32)
    if pieces:
        values = values * levels(key, dims, pieces, -0.22, 0.18)
    return jnp.clip(values, -reach, reach).astype(held_as)


def setup_inputs(seed: int = 0, part: int = 0) -> dict:
    key_of = jax.random.split(jax.random.key(seed), 7)
    part_splits = jax.random.split(jax.random.fold_in(key_of[6], part), 7)
    tokens = gaussian(part_splits[0], (TOKENS, D), 1.0, 6.0, ((0, 16),))
    grad_out = gaussian(part_splits[1], (TOKENS, D), 1.0, 6.0, ((0, 16),))
    gate_weight = gaussian(key_of[2], (D, FF), D ** -0.5, 0.09375, ((1, 16),))
    up_weight = gaussian(key_of[3], (D, FF), D ** -0.5, 0.09375, ((1, 16),))
    query_left = gaussian(key_of[4], (QUERIES, D, RANK), D ** -0.5, 0.09375, ((0, 16),))
    query_right = gaussian(key_of[5], (QUERIES, FF, RANK), (FF // 4) ** -0.5, 0.09375, ((0, 16),))
    return {"tokens": tokens, "grad_out": grad_out, "gate_weight": gate_weight, "up_weight": up_weight, "query_left": query_left, "query_right": query_right}


def reference(tokens, grad_out, gate_weight, up_weight, query_left, query_right):
    gate = jnp.dot(tokens, gate_weight, preferred_element_type=jnp.float32)
    up = jnp.dot(tokens, up_weight, preferred_element_type=jnp.float32)
    hidden = jax.nn.silu(gate) * up
    proj_right = jnp.einsum('tf,qfr->tqr', hidden, query_right.astype(jnp.float32), precision=lax.Precision.HIGHEST)
    proj_left = jnp.einsum('td,qdr->tqr', grad_out.astype(jnp.float32), query_left.astype(jnp.float32))
    return jnp.sum(proj_left * proj_right, axis=2)
```

```python
import jax
import jax.numpy as jnp
from jax import lax
from jax.sharding import PartitionSpec as P

AXIS = "query"
F32 = jnp.float32
BF16 = jnp.bfloat16


def swap(x, bit):
    n = lax.axis_size(AXIS)
    return lax.ppermute(x, AXIS, [(i, i ^ bit) for i in range(n)])


def pick(flag, when_zero, when_one):
    return jnp.where(flag == 0, when_zero, when_one)


def z_order(planes):
    order = [0]
    bit = planes // 2
    while bit >= 1:
        order = order + [k | bit for k in order]
        bit //= 2
    return order


def gather_rows(rows, core, planes):
    half = rows.shape[1] // 2
    mine = pick(core, rows[:, :half], rows[:, half:])
    theirs = pick(core, rows[:, half:], rows[:, :half])
    other = swap(theirs, 1)
    chip = pick(core, jnp.concatenate([mine, other]), jnp.concatenate([other, mine]))
    column = jnp.concatenate([chip if k == 0 else swap(chip, 4 * k) for k in z_order(planes)])
    both = jnp.concatenate([column, swap(column, 2)])
    rest = swap(both, 1)
    return pick(core, jnp.concatenate([both, rest], 1), jnp.concatenate([rest, both], 1))


def body(tokens, grad_out, gate_weight, up_weight, query_left, query_right):
    n = lax.axis_size(AXIS)
    planes = n // 4
    here = lax.axis_index(AXIS)
    core, y, z = here & 1, (here >> 1) & 1, here >> 2
    rank = query_right.shape[2]
    cols = gate_weight.shape[1]

    blocks = query_right[0].T.reshape(rank, n, cols).transpose(1, 0, 2)
    factors = lax.all_to_all(blocks, AXIS, split_axis=0, concat_axis=0, tiled=True)
    factors = factors.reshape(n // 2, 2, rank, cols)
    keep_factors = pick(core, factors[:, 0], factors[:, 1]).reshape(n // 2 * rank, cols)
    send_factors = pick(core, factors[:, 1], factors[:, 0]).reshape(n // 2 * rank, cols)

    whole = gather_rows(tokens, core, planes)
    grads = gather_rows(grad_out, core, planes)

    gate = jnp.dot(whole, gate_weight, preferred_element_type=F32)
    up = jnp.dot(whole, up_weight, preferred_element_type=F32)
    hidden = jax.nn.silu(gate) * up
    head = lax.reduce_precision(hidden, exponent_bits=8, mantissa_bits=7)
    high = head.astype(BF16)
    low = (hidden - head).astype(BF16)

    def project(with_factors):
        dims = (((1,), (1,)), ((), ()))
        return lax.dot_general(high, with_factors, dims, preferred_element_type=F32) + lax.dot_general(
            low, with_factors, dims, preferred_element_type=F32
        )

    left = jnp.dot(grads, query_left[0], preferred_element_type=F32)
    right = project(keep_factors) + swap(project(send_factors), 1)

    bit, place = 2, y
    while bit < n:
        half = right.shape[0] // 2
        right = right[:half] + swap(right[half:], bit)
        other = swap(left[half:], bit)
        left = pick(place, jnp.concatenate([left[:half], other], 1), jnp.concatenate([other, left[:half]], 1))
        bit *= 2
        place = (here // bit) & 1

    own = tokens.shape[0]
    spread = lax.broadcasted_iota(jnp.int32, (n // 2 * rank, n), 0) // rank * 2 + core
    spread = (spread == lax.broadcasted_iota(jnp.int32, (n // 2 * rank, n), 1)).astype(F32)
    sums = jnp.dot(left * right, spread, precision=lax.Precision.HIGHEST)
    return pick(core, sums[:own], sums[own:]) + swap(pick(core, sums[own:], sums[:own]), 1)


def solution(mesh):
    return jax.shard_map(
        body,
        mesh=mesh,
        in_specs=(
            P(("groups", "query"), None),
            P(("groups", "query"), None),
            P(None, "query"),
            P(None, "query"),
            P("query", None, None),
            P("query", None, None),
        ),
        out_specs=P(("groups", "query"), None),
        check_vma=False,
    )
```

```python
import functools

import jax
import jax.numpy as jnp
from jax import lax
from jax.experimental import pallas as pl
from jax.experimental.pallas import tpu as pltpu
from jax.sharding import PartitionSpec as P

AXIS = "query"
F32 = jnp.float32
BF16 = jnp.bfloat16
PAD = 16
LANES = 128


def swap(x, bit):
    n = lax.axis_size(AXIS)
    return lax.ppermute(x, AXIS, [(i, i ^ bit) for i in range(n)])


def pick(flag, when_zero, when_one):
    return jnp.where(flag == 0, when_zero, when_one)


def after(x, *others):
    return lax.optimization_barrier((x,) + others)[0]


def trade(x):
    return lax.all_to_all(x, AXIS, split_axis=0, concat_axis=0, tiled=True)


def nt_dot(a, b):
    return lax.dot_general(a, b, (((1,), (1,)), ((), ())), preferred_element_type=F32)


def z_order(planes):
    order = [0]
    bit = planes // 2
    while bit >= 1:
        order = order + [k | bit for k in order]
        bit //= 2
    return order


def row_offsets(n):
    return [(4 * k + 2 * y, c) for y in (0, 1) for k in z_order(n // 4) for c in (0, 1)]


def chip_rows(rows, core):
    half = rows.shape[1] // 2
    mine = pick(core, rows[:, :half], rows[:, half:])
    theirs = pick(core, rows[:, half:], rows[:, :half])
    other = swap(theirs, 1)
    return pick(core, jnp.concatenate([mine, other]), jnp.concatenate([other, mine]))


def group_rows(blocks, planes):
    column = jnp.concatenate([blocks[k] for k in z_order(planes)])
    both = jnp.concatenate([column, swap(column, 2)])
    return both, swap(both, 1)


def plain_hidden(core, own, other, gate_weight, up_weight):
    both = pick(core, jnp.concatenate([own, other], 1), jnp.concatenate([other, own], 1))
    gate = jnp.dot(both, gate_weight, preferred_element_type=F32)
    up = jnp.dot(both, up_weight, preferred_element_type=F32)
    hidden = jax.nn.silu(gate) * up
    head = lax.reduce_precision(hidden, exponent_bits=8, mantissa_bits=7)
    return head.astype(BF16), (hidden - head).astype(BF16)


class Layout:
    def __init__(self, n, cols, depth, rows, rank):
        self.n, self.cols, self.depth, self.rows, self.rank = n, cols, depth, rows, rank
        self.part = cols // LANES // 3 * LANES
        self.common = cols - 2 * self.part
        self.left = depth // 2
        self.wide = n // 2 * rank

    def fits(self, groups):
        return (
            groups % 2 == 0
            and self.cols % LANES == 0
            and self.part > 0
            and self.depth % (2 * LANES) == 0
            and self.depth // LANES * PAD <= self.rank
            and self.rows <= PAD
        )


def pack_kernel(lay, plane_ref, right_hbm, left_hbm, grad_hbm, split_ref, rest_ref, right_ref, left_ref, grad_ref, sems):
    copies = [
        pltpu.make_async_copy(source, to, sems.at[at])
        for at, (source, to) in enumerate(((right_hbm, right_ref), (left_hbm, left_ref), (grad_hbm, grad_ref)))
    ]
    for copy in copies:
        copy.start()
    for copy in copies:
        copy.wait()
    plane = plane_ref[0]
    cols, depth, part, common = lay.cols, lay.depth, lay.part, lay.common
    for to in range(lay.n):
        at = pl.multiple_of(to * cols + plane * part, LANES)
        split_ref[to, :, :part] = right_ref[:, pl.ds(at, part)]
        at = pl.multiple_of(to * depth + plane * lay.left, LANES)
        split_ref[to, :, part:] = left_ref[:, pl.ds(at, lay.left)]
        rest_ref[to, :, :common] = right_ref[:, to * cols + 2 * part : (to + 1) * cols]
        grad = grad_ref[:, to * depth : (to + 1) * depth].astype(F32)
        grad = jnp.concatenate([grad, jnp.zeros((PAD - lay.rows, depth), F32)]).astype(BF16)
        for piece in range(depth // LANES):
            rest_ref[to, piece * PAD : (piece + 1) * PAD, common:] = grad[:, piece * LANES : (piece + 1) * LANES]


def pack(lay, plane, right, left, grads):
    whole, away = pl.BlockSpec(memory_space=pltpu.VMEM), pl.BlockSpec(memory_space=pl.ANY)
    return pl.pallas_call(
        functools.partial(pack_kernel, lay),
        in_specs=[pl.BlockSpec(memory_space=pltpu.SMEM), away, away, away],
        out_specs=[whole, whole],
        out_shape=[
            jax.ShapeDtypeStruct((lay.n, lay.rank, lay.part + lay.left), BF16),
            jax.ShapeDtypeStruct((lay.n, lay.rank, lay.common + LANES), BF16),
        ],
        scratch_shapes=[pltpu.VMEM(x.shape, BF16) for x in (right, left, grads)] + [pltpu.SemaphoreType.DMA((3,))],
        compiler_params=pltpu.CompilerParams(vmem_limit_bytes=16 * 2**20),
        cost_estimate=pl.CostEstimate(flops=1000, bytes_accessed=1000, transcendentals=0),
        name="pack",
    )(plane.reshape(1), right, left, grads)


def hidden_kernel(steps, core_ref, own_ref, other_ref, gate_ref, up_ref, high_ref, low_ref, gate, up):
    step = pl.program_id(0)

    @pl.when(step == 0)
    def _():
        gate[...] = jnp.zeros_like(gate)
        up[...] = jnp.zeros_like(up)

    def add(rows_ref):
        rows = rows_ref[...]
        gate[...] += jnp.dot(rows, gate_ref[...], preferred_element_type=F32)
        up[...] += jnp.dot(rows, up_ref[...], preferred_element_type=F32)

    pl.when(step < steps)(lambda: add(own_ref))
    pl.when(step >= steps)(lambda: add(other_ref))

    @pl.when(step == 2 * steps - 1)
    def _():
        value = gate[...]
        hidden = value / (1.0 + jnp.exp(-value)) * up[...]
        high = hidden.astype(BF16)
        high_ref[...] = high
        low_ref[...] = (hidden - high.astype(F32)).astype(BF16)


def hidden_parts(core, own, other, gate_weight, up_weight):
    rows, half = own.shape
    cols = gate_weight.shape[1]
    steps = max(1, half // 512)
    step_rows = half // steps
    weight = pl.BlockSpec((step_rows, cols), lambda s, core_ref: ((core_ref[0] * steps + s) % (2 * steps), 0))
    out = pl.BlockSpec((rows, cols), lambda s, core_ref: (0, 0))
    return pl.pallas_call(
        functools.partial(hidden_kernel, steps),
        grid_spec=pltpu.PrefetchScalarGridSpec(
            num_scalar_prefetch=1,
            grid=(2 * steps,),
            in_specs=[
                pl.BlockSpec((rows, step_rows), lambda s, core_ref: (0, jnp.minimum(s, steps - 1))),
                pl.BlockSpec((rows, step_rows), lambda s, core_ref: (0, jnp.maximum(s - steps, 0))),
                weight,
                weight,
            ],
            out_specs=[out, out],
            scratch_shapes=[pltpu.VMEM((rows, cols), F32)] * 2,
        ),
        out_shape=[jax.ShapeDtypeStruct((rows, cols), BF16)] * 2,
        compiler_params=pltpu.CompilerParams(vmem_limit_bytes=48 * 2**20),
        cost_estimate=pl.CostEstimate(flops=1000, bytes_accessed=1000, transcendentals=0),
        name="hidden",
    )(core.reshape(1), own, other, gate_weight, up_weight)


def term_kernel(lay, at_ref, high_ref, low_ref, split_ref, twin_ref, rest_ref, keep_ref, send_ref, right, left, grad):
    here, plane = at_ref[0], at_ref[1]
    core = here & 1
    n, part, common, rank, rows, wide = lay.n, lay.part, lay.common, lay.rank, lay.rows, lay.wide
    for at, (offset, c) in enumerate(row_offsets(n)):
        source = ((here - core) ^ offset) + c
        for piece in range(lay.depth // LANES):
            grad[at * PAD : (at + 1) * PAD, piece * LANES : (piece + 1) * LANES] = rest_ref[
                source, piece * PAD : (piece + 1) * PAD, common:
            ]
    for turn, (out_ref, which) in enumerate(((send_ref, 1 - core), (keep_ref, core))):
        for pair in range(n // 2):
            query = 2 * pair + which
            block = slice(pair * rank, (pair + 1) * rank)
            halves = split_ref[query], twin_ref[query]
            for side in (0, 1):
                half = jnp.where(plane == side, halves[0], halves[1])
                right[turn, block, side * part : (side + 1) * part] = half[:, :part]
                left[turn, block, side * lay.left : (side + 1) * lay.left] = half[:, part:]
            right[turn, block, 2 * part :] = rest_ref[query, :, :common]
        out_ref[:, :wide] = nt_dot(high_ref[...], right[turn]) + nt_dot(low_ref[...], right[turn])
        padded = nt_dot(grad[...], left[turn])
        for at in range(n):
            out_ref[at * rows : (at + 1) * rows, wide:] = padded[at * PAD : at * PAD + rows]


def terms(lay, here, plane, high, low, split, twin, rest):
    whole = pl.BlockSpec(memory_space=pltpu.VMEM)
    return pl.pallas_call(
        functools.partial(term_kernel, lay),
        in_specs=[pl.BlockSpec(memory_space=pltpu.SMEM)] + [whole] * 5,
        out_specs=[whole, whole],
        out_shape=[jax.ShapeDtypeStruct((lay.n * lay.rows, 2 * lay.wide), F32)] * 2,
        scratch_shapes=[
            pltpu.VMEM((2, lay.wide, lay.cols), BF16),
            pltpu.VMEM((2, lay.wide, lay.depth), BF16),
            pltpu.VMEM((lay.n * PAD, lay.depth), BF16),
        ],
        compiler_params=pltpu.CompilerParams(vmem_limit_bytes=24 * 2**20),
        name="terms",
    )(jnp.stack([here, plane]), high, low, split, twin, rest)


def plain_terms(here, high, low, right, left, grads):
    n, rank = right.shape[:2]
    core = here & 1
    sources = [((here - core) ^ offset) + c for offset, c in row_offsets(n)]
    grads = jnp.concatenate([lax.dynamic_index_in_dim(grads, source, keepdims=False) for source in sources])
    outs = []
    for which in (core, 1 - core):
        some = lambda x: pick(which, *jnp.moveaxis(x.reshape(n // 2, 2, rank, -1), 1, 0)).reshape(n // 2 * rank, -1)
        some_right, some_left = some(right), some(left)
        outs.append(jnp.concatenate([nt_dot(high, some_right) + nt_dot(low, some_right), nt_dot(grads, some_left)], 1))
    return outs


def body(tokens, grad_out, gate_weight, up_weight, query_left, query_right):
    n = lax.axis_size(AXIS)
    planes = n // 4
    here = lax.axis_index(AXIS)
    core = here & 1
    own, width = tokens.shape
    rank = query_right.shape[2]
    cols = gate_weight.shape[1]
    depth = width // n
    right_own, left_own = query_right[0].T, query_left[0].T
    lay = Layout(n, cols, width // n, own, rank)
    fits = lay.fits(lax.axis_size("groups"))

    chip = chip_rows(tokens, core)
    blocks = {0: chip}
    for k in range(1, planes):
        blocks[k] = swap(chip, 4 * k)

    if fits:
        plane = lax.axis_index("groups") & 1
        split, rest = pack(lay, plane, right_own, left_own, grad_out)
        split = trade(after(split, blocks[1]))
        rest = trade(after(rest, *blocks.values()))
        groups = lax.axis_size("groups")
        twin = lax.ppermute(split, "groups", [(g, g ^ 1) for g in range(groups)])
    else:
        cut = lambda x: x.reshape(x.shape[0], n, -1).transpose(1, 0, 2)
        right_all, left_all, grad_all = (trade(cut(x)) for x in (right_own, left_own, grad_out))

    own_half, other_half = group_rows(blocks, planes)
    if fits:
        high, low = hidden_parts(core, own_half, other_half, gate_weight, up_weight)
        keep, send = terms(lay, here, plane, high, low, split, twin, rest)
    else:
        high, low = plain_hidden(core, own_half, other_half, gate_weight, up_weight)
        keep, send = plain_terms(here, high, low, right_all, left_all, grad_all)

    sums = keep + swap(send, 1)
    bit = 2
    while bit < n:
        half = sums.shape[0] // 2
        sums = sums[:half] + swap(sums[half:], bit)
        bit *= 2

    wide = n // 2 * rank
    spread = lax.broadcasted_iota(jnp.int32, (wide, n), 0) // rank * 2 + core
    spread = (spread == lax.broadcasted_iota(jnp.int32, (wide, n), 1)).astype(F32)
    scores = jnp.dot(sums[:, :wide] * sums[:, wide:], spread, precision=lax.Precision.HIGHEST)
    return pick(core, scores[:own], scores[own:]) + swap(pick(core, scores[own:], scores[:own]), 1)


def solution(mesh):
    return jax.shard_map(
        body,
        mesh=mesh,
        in_specs=(
            P(("groups", "query"), None),
            P(("groups", "query"), None),
            P(None, "query"),
            P(None, "query"),
            P("query", None, None),
            P("query", None, None),
        ),
        out_specs=P(("groups", "query"), None),
        check_vma=False,
    )
```

```python
import functools

import jax
import jax.numpy as jnp
from jax import lax
from jax.experimental import pallas as pl
from jax.experimental.pallas import tpu as pltpu
from jax.sharding import PartitionSpec as P

AXIS = "query"
F32 = jnp.float32
BF16 = jnp.bfloat16
PAD = 16
LANES = 128


def swap(x, bit):
    n = lax.axis_size(AXIS)
    return lax.ppermute(x, AXIS, [(i, i ^ bit) for i in range(n)])


def pick(flag, when_zero, when_one):
    return jnp.where(flag == 0, when_zero, when_one)


def after(x, *others):
    return lax.optimization_barrier((x,) + others)[0]


def trade(x):
    return lax.all_to_all(x, AXIS, split_axis=0, concat_axis=0, tiled=True)


def nt_dot(a, b):
    return lax.dot_general(a, b, (((1,), (1,)), ((), ())), preferred_element_type=F32)


def z_order(planes):
    order = [0]
    bit = planes // 2
    while bit >= 1:
        order = order + [k | bit for k in order]
        bit //= 2
    return order


def row_offsets(n):
    return [(4 * k + 2 * y, c) for y in (0, 1) for k in z_order(n // 4) for c in (0, 1)]


def chip_rows(rows, core, also):
    half = rows.shape[1] // 2
    mine = pick(core, rows[:, :half], rows[:, half:])
    theirs = pick(core, rows[:, half:], rows[:, :half])
    other = after(swap(theirs, 1), *also)
    return pick(core, jnp.concatenate([mine, other]), jnp.concatenate([other, mine]))


def group_rows(blocks, planes):
    column = jnp.concatenate([blocks[k] for k in z_order(planes)])
    both = jnp.concatenate([column, swap(column, 2)])
    return both, swap(both, 1)


def plain_hidden(core, own, other, gate_weight, up_weight):
    both = pick(core, jnp.concatenate([own, other], 1), jnp.concatenate([other, own], 1))
    gate = jnp.dot(both, gate_weight, preferred_element_type=F32)
    up = jnp.dot(both, up_weight, preferred_element_type=F32)
    hidden = jax.nn.silu(gate) * up
    head = lax.reduce_precision(hidden, exponent_bits=8, mantissa_bits=7)
    return head.astype(BF16), (hidden - head).astype(BF16)


class Layout:
    def __init__(self, n, cols, depth, rows, rank):
        self.n, self.cols, self.depth, self.rows, self.rank = n, cols, depth, rows, rank
        self.part = cols // LANES // 3 * LANES
        self.common = cols - 2 * self.part
        self.left = depth // 2
        self.wide = n * rank

    def fits(self, groups):
        return (
            groups % 2 == 0
            and self.cols % LANES == 0
            and self.part > 0
            and self.depth % (2 * LANES) == 0
            and self.depth // LANES * PAD <= self.rank
            and self.rows <= PAD
            and self.n % 16 == 0
        )


def pack_kernel(lay, plane_ref, right_hbm, left_hbm, grad_hbm, split_ref, rest_ref, right_ref, left_ref, grad_ref, sems):
    copies = [
        pltpu.make_async_copy(source, to, sems.at[at])
        for at, (source, to) in enumerate(((right_hbm, right_ref), (left_hbm, left_ref), (grad_hbm, grad_ref)))
    ]
    for copy in copies:
        copy.start()
    for copy in copies:
        copy.wait()
    plane = plane_ref[0]
    cols, depth, part, common = lay.cols, lay.depth, lay.part, lay.common
    for to in range(lay.n):
        at = pl.multiple_of(to * cols + plane * part, LANES)
        split_ref[to, :, :part] = right_ref[:, pl.ds(at, part)]
        at = pl.multiple_of(to * depth + plane * lay.left, LANES)
        split_ref[to, :, part:] = left_ref[:, pl.ds(at, lay.left)]
        rest_ref[to, :, :common] = right_ref[:, to * cols + 2 * part : (to + 1) * cols]
        grad = grad_ref[:, to * depth : (to + 1) * depth].astype(F32)
        grad = jnp.concatenate([grad, jnp.zeros((PAD - lay.rows, depth), F32)]).astype(BF16)
        for piece in range(depth // LANES):
            rest_ref[to, piece * PAD : (piece + 1) * PAD, common:] = grad[:, piece * LANES : (piece + 1) * LANES]


def pack(lay, plane, right, left, grads):
    whole, away = pl.BlockSpec(memory_space=pltpu.VMEM), pl.BlockSpec(memory_space=pl.ANY)
    return pl.pallas_call(
        functools.partial(pack_kernel, lay),
        in_specs=[pl.BlockSpec(memory_space=pltpu.SMEM), away, away, away],
        out_specs=[whole, whole],
        out_shape=[
            jax.ShapeDtypeStruct((lay.n, lay.rank, lay.part + lay.left), BF16),
            jax.ShapeDtypeStruct((lay.n, lay.rank, lay.common + LANES), BF16),
        ],
        scratch_shapes=[pltpu.VMEM(x.shape, BF16) for x in (right, left, grads)] + [pltpu.SemaphoreType.DMA((3,))],
        compiler_params=pltpu.CompilerParams(vmem_limit_bytes=56 * 2**20),
        cost_estimate=pl.CostEstimate(flops=1000, bytes_accessed=1000, transcendentals=0),
        name="pack",
    )(plane.reshape(1), right, left, grads)


def hidden_kernel(steps, core_ref, own_ref, other_ref, gate_ref, up_ref, high_ref, low_ref, gate, up):
    step = pl.program_id(0)

    @pl.when(step == 0)
    def _():
        gate[...] = jnp.zeros_like(gate)
        up[...] = jnp.zeros_like(up)

    def add(rows_ref):
        rows = rows_ref[...]
        gate[...] += jnp.dot(rows, gate_ref[...], preferred_element_type=F32)
        up[...] += jnp.dot(rows, up_ref[...], preferred_element_type=F32)

    pl.when(step < steps)(lambda: add(own_ref))
    pl.when(step >= steps)(lambda: add(other_ref))

    @pl.when(step == 2 * steps - 1)
    def _():
        value = gate[...]
        hidden = value / (1.0 + jnp.exp(-value)) * up[...]
        high = hidden.astype(BF16)
        high_ref[...] = high
        low_ref[...] = (hidden - high.astype(F32)).astype(BF16)


def hidden_parts(core, own, other, gate_weight, up_weight):
    rows, half = own.shape
    cols = gate_weight.shape[1]
    steps = max(1, half // 512)
    step_rows = half // steps
    weight = pl.BlockSpec((step_rows, cols), lambda s, core_ref: ((core_ref[0] * steps + s) % (2 * steps), 0))
    out = pl.BlockSpec((rows, cols), lambda s, core_ref: (0, 0))
    return pl.pallas_call(
        functools.partial(hidden_kernel, steps),
        grid_spec=pltpu.PrefetchScalarGridSpec(
            num_scalar_prefetch=1,
            grid=(2 * steps,),
            in_specs=[
                pl.BlockSpec((rows, step_rows), lambda s, core_ref: (0, jnp.minimum(s, steps - 1))),
                pl.BlockSpec((rows, step_rows), lambda s, core_ref: (0, jnp.maximum(s - steps, 0))),
                weight,
                weight,
            ],
            out_specs=[out, out],
            scratch_shapes=[pltpu.VMEM((rows, cols), F32)] * 2,
        ),
        out_shape=[jax.ShapeDtypeStruct((rows, cols), BF16)] * 2,
        compiler_params=pltpu.CompilerParams(vmem_limit_bytes=48 * 2**20),
        cost_estimate=pl.CostEstimate(flops=1000, bytes_accessed=1000, transcendentals=0),
        name="hidden",
    )(core.reshape(1), own, other, gate_weight, up_weight)


def term_kernel(lay, at_ref, high_ref, low_ref, split_ref, twin_ref, rest_ref, *more):
    keep_ref, send_ref, keep_left_ref, send_left_ref, right, left, grad = more
    here, plane = at_ref[0], at_ref[1]
    core = here & 1
    n, part, common, rank, rows, wide = lay.n, lay.part, lay.common, lay.rank, lay.rows, lay.wide
    for at, (offset, c) in enumerate(row_offsets(n)):
        source = ((here - core) ^ offset) + c
        for piece in range(lay.depth // LANES):
            grad[at * PAD : (at + 1) * PAD, piece * LANES : (piece + 1) * LANES] = rest_ref[
                source, piece * PAD : (piece + 1) * PAD, common:
            ]
    for turn in (0, 1):
        for at in range(n // 2):
            query = turn * (n // 2) + at
            block = slice(query * rank, (query + 1) * rank)
            for side in (0, 1):
                half = jnp.where(plane == side, split_ref[query], twin_ref[query])
                right[block, side * part : (side + 1) * part] = half[:, :part]
                left[block, side * lay.left : (side + 1) * lay.left] = half[:, part:]
            right[block, 2 * part :] = rest_ref[query, :, :common]
        block = slice(turn * wide // 2, (turn + 1) * wide // 2)
        rights = nt_dot(high_ref[...], right[block]) + nt_dot(low_ref[...], right[block])
        lefts = nt_dot(grad[...], left[block])
        for pair in range(n // 2):
            to = slice(pair * rows, (pair + 1) * rows)
            first, second = rights[2 * pair * rows :][:rows], rights[(2 * pair + 1) * rows :][:rows]
            keep_ref[to, block] = jnp.where(core == 0, first, second)
            send_ref[to, block] = jnp.where(core == 0, second, first)
            quarter = n // 8
            at = (pair // quarter & 1) * 2 * quarter + (pair // quarter >> 1) * quarter + pair % quarter
            to = slice(at * rows, (at + 1) * rows)
            first, second = lefts[2 * pair * PAD :][:rows], lefts[(2 * pair + 1) * PAD :][:rows]
            keep_left_ref[to, block] = jnp.where(core == 0, first, second)
            send_left_ref[to, block] = jnp.where(core == 0, second, first)


def terms(lay, here, plane, high, low, split, twin, rest):
    whole = pl.BlockSpec(memory_space=pltpu.VMEM)
    return pl.pallas_call(
        functools.partial(term_kernel, lay),
        in_specs=[pl.BlockSpec(memory_space=pltpu.SMEM)] + [whole] * 5,
        out_specs=[whole] * 4,
        out_shape=[jax.ShapeDtypeStruct((lay.n // 2 * lay.rows, lay.wide), F32)] * 4,
        scratch_shapes=[
            pltpu.VMEM((lay.wide, lay.cols), BF16),
            pltpu.VMEM((lay.wide, lay.depth), BF16),
            pltpu.VMEM((lay.n * PAD, lay.depth), BF16),
        ],
        compiler_params=pltpu.CompilerParams(vmem_limit_bytes=24 * 2**20),
        name="terms",
    )(jnp.stack([here, plane]), high, low, split, twin, rest)


def plain_terms(here, high, low, right, left, grads):
    n, rank = right.shape[:2]
    rows = grads.shape[1]
    core = here & 1
    sources = [((here - core) ^ offset) + c for offset, c in row_offsets(n)]
    grads = jnp.concatenate([lax.dynamic_index_in_dim(grads, source, keepdims=False) for source in sources])
    right, left = right.reshape(n * rank, -1), left.reshape(n * rank, -1)
    both = jnp.concatenate([nt_dot(high, right) + nt_dot(low, right), nt_dot(grads, left)], 1)
    both = both.reshape(n // 2, 2, rows, -1)
    outs = pick(core, both[:, 0], both[:, 1]), pick(core, both[:, 1], both[:, 0])
    return [out.reshape(n // 2 * rows, -1) for out in outs]


def spread(wide, n):
    query = lax.broadcasted_iota(jnp.int32, (wide, n), 0) // (wide // n)
    return (query == lax.broadcasted_iota(jnp.int32, (wide, n), 1)).astype(F32)


def score_kernel(n, right_ref, other_right_ref, left_ref, other_left_ref, out_ref):
    rows, wide = other_right_ref.shape
    products = (right_ref[:rows] + other_right_ref[...]) * (left_ref[:rows] + other_left_ref[...])
    out_ref[...] = jnp.dot(
        products, spread(wide, n), precision=lax.Precision.HIGHEST, preferred_element_type=F32
    )


def score(n, right, other_right, left, other_left):
    whole = pl.BlockSpec(memory_space=pltpu.VMEM)
    return pl.pallas_call(
        functools.partial(score_kernel, n),
        in_specs=[whole] * 4,
        out_specs=whole,
        out_shape=jax.ShapeDtypeStruct((other_right.shape[0], n), F32),
        compiler_params=pltpu.CompilerParams(vmem_limit_bytes=8 * 2**20),
        name="score",
    )(right, other_right, left, other_left)


def halve(sums, bit):
    half = sums.shape[0] // 2
    return sums[:half] + swap(sums[half:], bit)


def body(tokens, grad_out, gate_weight, up_weight, query_left, query_right):
    n = lax.axis_size(AXIS)
    planes = n // 4
    here = lax.axis_index(AXIS)
    core = here & 1
    own, width = tokens.shape
    rank = query_right.shape[2]
    cols = gate_weight.shape[1]
    depth = width // n
    right_own, left_own = query_right[0].T, query_left[0].T
    lay = Layout(n, cols, width // n, own, rank)
    fits = lay.fits(lax.axis_size("groups"))

    plane = lax.axis_index("groups") & 1
    also = ()
    if fits:
        split, rest = also = pack(lay, plane, right_own, left_own, grad_out)
    chip = chip_rows(tokens, core, also)
    blocks = {0: chip}
    for k in range(1, planes):
        blocks[k] = swap(chip, 4 * k)

    if fits:
        split = trade(after(split, blocks[1]))
        rest = trade(after(rest, *blocks.values()))
        groups = lax.axis_size("groups")
        twin = lax.ppermute(split, "groups", [(g, g ^ 1) for g in range(groups)])
    else:
        cut = lambda x: x.reshape(x.shape[0], n, -1).transpose(1, 0, 2)
        right_all, left_all, grad_all = (trade(cut(x)) for x in (right_own, left_own, grad_out))

    own_half, other_half = group_rows(blocks, planes)
    if fits:
        high, low = hidden_parts(core, own_half, other_half, gate_weight, up_weight)
        keep, send, keep_left, send_left = terms(lay, here, plane, high, low, split, twin, rest)
        right, left = keep + swap(send, 1), keep_left + swap(send_left, 1)
        right, left = halve(right, 2), halve(left, 4)
        right, left = halve(right, 4), halve(left, 2)
        bit = 8
        while 2 * bit < n:
            right, left = halve(right, bit), halve(left, bit)
            bit *= 2
        return score(n, right, swap(right[own:], bit), left, swap(left[own:], bit))

    high, low = plain_hidden(core, own_half, other_half, gate_weight, up_weight)
    keep, send = plain_terms(here, high, low, right_all, left_all, grad_all)

    sums = keep + swap(send, 1)
    bit = 2
    while bit < n:
        sums = halve(sums, bit)
        bit *= 2
    wide = n * rank
    return jnp.dot(sums[:, :wide] * sums[:, wide:], spread(wide, n), precision=lax.Precision.HIGHEST)


def solution(mesh):
    return jax.shard_map(
        body,
        mesh=mesh,
        in_specs=(
            P(("groups", "query"), None),
            P(("groups", "query"), None),
            P(None, "query"),
            P(None, "query"),
            P("query", None, None),
            P("query", None, None),
        ),
        out_specs=P(("groups", "query"), None),
        check_vma=False,
    )
```

```python
import functools

import jax
import jax.numpy as jnp
from jax import lax
from jax.experimental import pallas as pl
from jax.experimental.pallas import tpu as pltpu
from jax.sharding import PartitionSpec as P

AXIS = "query"
F32 = jnp.float32
BF16 = jnp.bfloat16
PAD = 16
LANES = 128


def swap(x, bit):
    n = lax.axis_size(AXIS)
    return lax.ppermute(x, AXIS, [(i, i ^ bit) for i in range(n)])


def pick(flag, when_zero, when_one):
    return jnp.where(flag == 0, when_zero, when_one)


def after(x, *others):
    return lax.optimization_barrier((x,) + others)[0]


def trade(x):
    return lax.all_to_all(x, AXIS, split_axis=0, concat_axis=0, tiled=True)


def nt_dot(a, b):
    return lax.dot_general(a, b, (((1,), (1,)), ((), ())), preferred_element_type=F32)


def z_order(planes):
    order = [0]
    bit = planes // 2
    while bit >= 1:
        order = order + [k | bit for k in order]
        bit //= 2
    return order


def row_offsets(n):
    return [(4 * k + 2 * y, c) for y in (0, 1) for k in z_order(n // 4) for c in (0, 1)]


def chip_rows(rows, core, also):
    half = rows.shape[1] // 2
    mine = pick(core, rows[:, :half], rows[:, half:])
    theirs = pick(core, rows[:, half:], rows[:, :half])
    other = after(swap(theirs, 1), *also)
    return pick(core, jnp.concatenate([mine, other]), jnp.concatenate([other, mine]))


def group_rows(blocks, planes):
    column = same(jnp.concatenate([blocks[k] for k in z_order(planes)]))
    both = jnp.concatenate([column, swap(column, 2)])
    return both, swap(both, 1)


def plain_hidden(core, own, other, gate_weight, up_weight):
    both = pick(core, jnp.concatenate([own, other], 1), jnp.concatenate([other, own], 1))
    gate = jnp.dot(both, gate_weight, preferred_element_type=F32)
    up = jnp.dot(both, up_weight, preferred_element_type=F32)
    hidden = jax.nn.silu(gate) * up
    head = lax.reduce_precision(hidden, exponent_bits=8, mantissa_bits=7)
    return head.astype(BF16), (hidden - head).astype(BF16)


class Layout:
    def __init__(self, n, cols, depth, rows, rank):
        self.n, self.cols, self.depth, self.rows, self.rank = n, cols, depth, rows, rank
        self.part = cols // LANES // 3 * LANES
        self.common = cols - 2 * self.part
        self.left = depth // 2
        self.wide = n * rank

    def fits(self, groups):
        return (
            groups % 2 == 0
            and self.cols % LANES == 0
            and self.part > 0
            and self.depth % (2 * LANES) == 0
            and self.depth // LANES * PAD <= self.rank
            and self.rows <= PAD
            and self.n % 16 == 0
        )


def pack_kernel(lay, plane_ref, right_hbm, left_hbm, grad_hbm, split_ref, rest_ref, right_ref, left_ref, grad_ref, sems):
    copies = [
        pltpu.make_async_copy(source, to, sems.at[at])
        for at, (source, to) in enumerate(((right_hbm, right_ref), (left_hbm, left_ref), (grad_hbm, grad_ref)))
    ]
    for copy in copies:
        copy.start()
    for copy in copies:
        copy.wait()
    plane = plane_ref[0]
    cols, depth, part, common = lay.cols, lay.depth, lay.part, lay.common
    for to in range(lay.n):
        at = pl.multiple_of(to * cols + plane * part, LANES)
        split_ref[to, :, :part] = right_ref[:, pl.ds(at, part)]
        at = pl.multiple_of(to * depth + plane * lay.left, LANES)
        split_ref[to, :, part:] = left_ref[:, pl.ds(at, lay.left)]
        rest_ref[to, :, :common] = right_ref[:, to * cols + 2 * part : (to + 1) * cols]
        grad = grad_ref[:, to * depth : (to + 1) * depth].astype(F32)
        grad = jnp.concatenate([grad, jnp.zeros((PAD - lay.rows, depth), F32)]).astype(BF16)
        for piece in range(depth // LANES):
            rest_ref[to, piece * PAD : (piece + 1) * PAD, common:] = grad[:, piece * LANES : (piece + 1) * LANES]


def pack(lay, plane, right, left, grads):
    whole, away = pl.BlockSpec(memory_space=pltpu.VMEM), pl.BlockSpec(memory_space=pl.ANY)
    return pl.pallas_call(
        functools.partial(pack_kernel, lay),
        in_specs=[pl.BlockSpec(memory_space=pltpu.SMEM), away, away, away],
        out_specs=[whole, whole],
        out_shape=[
            jax.ShapeDtypeStruct((lay.n, lay.rank, lay.part + lay.left), BF16),
            jax.ShapeDtypeStruct((lay.n, lay.rank, lay.common + LANES), BF16),
        ],
        scratch_shapes=[pltpu.VMEM(x.shape, BF16) for x in (right, left, grads)] + [pltpu.SemaphoreType.DMA((3,))],
        compiler_params=pltpu.CompilerParams(vmem_limit_bytes=56 * 2**20),
        cost_estimate=pl.CostEstimate(flops=1000, bytes_accessed=1000, transcendentals=0),
        name="pack",
    )(plane.reshape(1), right, left, grads)


def same_kernel(x_ref, out_ref):
    out_ref[...] = x_ref[...]


def same(x):
    whole = pl.BlockSpec(memory_space=pltpu.VMEM)
    return pl.pallas_call(
        same_kernel,
        in_specs=[whole],
        out_specs=whole,
        out_shape=jax.ShapeDtypeStruct(x.shape, x.dtype),
        compiler_params=pltpu.CompilerParams(vmem_limit_bytes=4 * 2**20),
        cost_estimate=pl.CostEstimate(flops=10_000_000_000, bytes_accessed=1000, transcendentals=0),
        name="same",
    )(x)


def hidden_kernel(steps, core_ref, own_ref, other_ref, gate_ref, up_ref, high_ref, low_ref, gate, up):
    step = pl.program_id(0)

    @pl.when(step == 0)
    def _():
        gate[...] = jnp.zeros_like(gate)
        up[...] = jnp.zeros_like(up)

    def add(rows_ref):
        rows = rows_ref[...]
        gate[...] += jnp.dot(rows, gate_ref[...], preferred_element_type=F32)
        up[...] += jnp.dot(rows, up_ref[...], preferred_element_type=F32)

    pl.when(step < steps)(lambda: add(own_ref))
    pl.when(step >= steps)(lambda: add(other_ref))

    @pl.when(step == 2 * steps - 1)
    def _():
        value = gate[...]
        hidden = value / (1.0 + jnp.exp(-value)) * up[...]
        high = hidden.astype(BF16)
        high_ref[...] = high
        low_ref[...] = (hidden - high.astype(F32)).astype(BF16)


def hidden_parts(core, own, other, gate_weight, up_weight):
    rows, half = own.shape
    cols = gate_weight.shape[1]
    steps = max(1, half // 1024)
    step_rows = half // steps
    weight = pl.BlockSpec((step_rows, cols), lambda s, core_ref: ((core_ref[0] * steps + s) % (2 * steps), 0))
    out = pl.BlockSpec((rows, cols), lambda s, core_ref: (0, 0))
    return pl.pallas_call(
        functools.partial(hidden_kernel, steps),
        grid_spec=pltpu.PrefetchScalarGridSpec(
            num_scalar_prefetch=1,
            grid=(2 * steps,),
            in_specs=[
                pl.BlockSpec((rows, step_rows), lambda s, core_ref: (0, jnp.minimum(s, steps - 1))),
                pl.BlockSpec((rows, step_rows), lambda s, core_ref: (0, jnp.maximum(s - steps, 0))),
                weight,
                weight,
            ],
            out_specs=[out, out],
            scratch_shapes=[pltpu.VMEM((rows, cols), F32)] * 2,
        ),
        out_shape=[jax.ShapeDtypeStruct((rows, cols), BF16)] * 2,
        compiler_params=pltpu.CompilerParams(vmem_limit_bytes=48 * 2**20),
        cost_estimate=pl.CostEstimate(flops=1000, bytes_accessed=1000, transcendentals=0),
        name="hidden",
    )(core.reshape(1), own, other, gate_weight, up_weight)


def term_kernel(lay, at_ref, high_ref, low_ref, split_ref, twin_ref, rest_ref, *more):
    keep_ref, send_ref, keep_left_ref, send_left_ref, right, left, grad = more
    here, plane = at_ref[0], at_ref[1]
    core = here & 1
    n, part, common, rank, rows, wide = lay.n, lay.part, lay.common, lay.rank, lay.rows, lay.wide
    for at, (offset, c) in enumerate(row_offsets(n)):
        source = ((here - core) ^ offset) + c
        for piece in range(lay.depth // LANES):
            grad[at * PAD : (at + 1) * PAD, piece * LANES : (piece + 1) * LANES] = rest_ref[
                source, piece * PAD : (piece + 1) * PAD, common:
            ]
    for turn in (0, 1):
        for at in range(n // 2):
            query = turn * (n // 2) + at
            block = slice(query * rank, (query + 1) * rank)
            for side in (0, 1):
                half = jnp.where(plane == side, split_ref[query], twin_ref[query])
                right[block, side * part : (side + 1) * part] = half[:, :part]
                left[block, side * lay.left : (side + 1) * lay.left] = half[:, part:]
            right[block, 2 * part :] = rest_ref[query, :, :common]
        block = slice(turn * wide // 2, (turn + 1) * wide // 2)
        rights = nt_dot(high_ref[...], right[block]) + nt_dot(low_ref[...], right[block])
        lefts = nt_dot(grad[...], left[block])
        for pair in range(n // 2):
            to = slice(pair * rows, (pair + 1) * rows)
            first, second = rights[2 * pair * rows :][:rows], rights[(2 * pair + 1) * rows :][:rows]
            keep_ref[to, block] = jnp.where(core == 0, first, second)
            send_ref[to, block] = jnp.where(core == 0, second, first)
            quarter = n // 8
            at = (pair // quarter & 1) * 2 * quarter + (pair // quarter >> 1) * quarter + pair % quarter
            to = slice(at * rows, (at + 1) * rows)
            first, second = lefts[2 * pair * PAD :][:rows], lefts[(2 * pair + 1) * PAD :][:rows]
            keep_left_ref[to, block] = jnp.where(core == 0, first, second)
            send_left_ref[to, block] = jnp.where(core == 0, second, first)


def terms(lay, here, plane, high, low, split, twin, rest):
    whole = pl.BlockSpec(memory_space=pltpu.VMEM)
    return pl.pallas_call(
        functools.partial(term_kernel, lay),
        in_specs=[pl.BlockSpec(memory_space=pltpu.SMEM)] + [whole] * 5,
        out_specs=[whole] * 4,
        out_shape=[jax.ShapeDtypeStruct((lay.n // 2 * lay.rows, lay.wide), F32)] * 4,
        scratch_shapes=[
            pltpu.VMEM((lay.wide, lay.cols), BF16),
            pltpu.VMEM((lay.wide, lay.depth), BF16),
            pltpu.VMEM((lay.n * PAD, lay.depth), BF16),
        ],
        compiler_params=pltpu.CompilerParams(vmem_limit_bytes=24 * 2**20),
        name="terms",
    )(jnp.stack([here, plane]), high, low, split, twin, rest)


def plain_terms(here, high, low, right, left, grads):
    n, rank = right.shape[:2]
    rows = grads.shape[1]
    core = here & 1
    sources = [((here - core) ^ offset) + c for offset, c in row_offsets(n)]
    grads = jnp.concatenate([lax.dynamic_index_in_dim(grads, source, keepdims=False) for source in sources])
    right, left = right.reshape(n * rank, -1), left.reshape(n * rank, -1)
    both = jnp.concatenate([nt_dot(high, right) + nt_dot(low, right), nt_dot(grads, left)], 1)
    both = both.reshape(n // 2, 2, rows, -1)
    outs = pick(core, both[:, 0], both[:, 1]), pick(core, both[:, 1], both[:, 0])
    return [out.reshape(n // 2 * rows, -1) for out in outs]


def spread(wide, n):
    query = lax.broadcasted_iota(jnp.int32, (wide, n), 0) // (wide // n)
    return (query == lax.broadcasted_iota(jnp.int32, (wide, n), 1)).astype(F32)


def score_kernel(n, right_ref, left_ref, other_ref, out_ref):
    rows, wide = other_ref.shape[0], right_ref.shape[1]
    products = (right_ref[:rows] + other_ref[:, :wide]) * (left_ref[:rows] + other_ref[:, wide:])
    out_ref[...] = jnp.dot(
        products, spread(wide, n), precision=lax.Precision.HIGHEST, preferred_element_type=F32
    )


def score(n, right, left, other):
    whole = pl.BlockSpec(memory_space=pltpu.VMEM)
    return pl.pallas_call(
        functools.partial(score_kernel, n),
        in_specs=[whole] * 3,
        out_specs=whole,
        out_shape=jax.ShapeDtypeStruct((other.shape[0], n), F32),
        compiler_params=pltpu.CompilerParams(vmem_limit_bytes=8 * 2**20),
        name="score",
    )(right, left, other)


def halve(sums, bit):
    half = sums.shape[0] // 2
    return sums[:half] + swap(sums[half:], bit)


def body(tokens, grad_out, gate_weight, up_weight, query_left, query_right):
    n = lax.axis_size(AXIS)
    planes = n // 4
    here = lax.axis_index(AXIS)
    core = here & 1
    own, width = tokens.shape
    rank = query_right.shape[2]
    cols = gate_weight.shape[1]
    depth = width // n
    right_own, left_own = query_right[0].T, query_left[0].T
    lay = Layout(n, cols, width // n, own, rank)
    fits = lay.fits(lax.axis_size("groups"))

    plane = lax.axis_index("groups") & 1
    also = ()
    if fits:
        split, rest = also = pack(lay, plane, right_own, left_own, grad_out)
    chip = chip_rows(tokens, core, also)
    blocks = {0: chip}
    for k in range(1, planes):
        blocks[k] = swap(chip, 4 * k)

    if fits:
        split = trade(after(split, chip))
        rest = trade(after(rest, *blocks.values()))
        groups = lax.axis_size("groups")
        twin = lax.ppermute(split, "groups", [(g, g ^ 1) for g in range(groups)])
    else:
        cut = lambda x: x.reshape(x.shape[0], n, -1).transpose(1, 0, 2)
        right_all, left_all, grad_all = (trade(cut(x)) for x in (right_own, left_own, grad_out))

    own_half, other_half = group_rows(blocks, planes)
    if fits:
        high, low = hidden_parts(core, own_half, other_half, gate_weight, up_weight)
        keep, send, keep_left, send_left = terms(lay, here, plane, high, low, split, twin, rest)
        right, left = keep + swap(send, 1), keep_left + swap(send_left, 1)
        right, left = halve(right, 2), halve(left, 4)
        right, left = halve(right, 4), halve(left, 2)
        bit = 8
        while 2 * bit < n:
            right, left = halve(right, bit), halve(left, bit)
            bit *= 2
        other = swap(jnp.concatenate([right[own:], left[own:]], 1), bit)
        return score(n, right, left, other)

    high, low = plain_hidden(core, own_half, other_half, gate_weight, up_weight)
    keep, send = plain_terms(here, high, low, right_all, left_all, grad_all)

    sums = keep + swap(send, 1)
    bit = 2
    while bit < n:
        sums = halve(sums, bit)
        bit *= 2
    wide = n * rank
    return jnp.dot(sums[:, :wide] * sums[:, wide:], spread(wide, n), precision=lax.Precision.HIGHEST)


def solution(mesh):
    return jax.shard_map(
        body,
        mesh=mesh,
        in_specs=(
            P(("groups", "query"), None),
            P(("groups", "query"), None),
            P(None, "query"),
            P(None, "query"),
            P("query", None, None),
            P("query", None, None),
        ),
        out_specs=P(("groups", "query"), None),
        check_vma=False,
    )
```

```python
import functools

import jax
import jax.numpy as jnp
from jax import lax
from jax.experimental import pallas as pl
from jax.experimental.pallas import tpu as pltpu
from jax.sharding import PartitionSpec as P

AXIS = "query"
F32 = jnp.float32
BF16 = jnp.bfloat16
PAD = 16
LANES = 128


def swap(x, bit):
    n = lax.axis_size(AXIS)
    return lax.ppermute(x, AXIS, [(i, i ^ bit) for i in range(n)])


def pick(flag, when_zero, when_one):
    return jnp.where(flag == 0, when_zero, when_one)


def after(x, *others):
    return lax.optimization_barrier((x,) + others)[0]


def trade(x):
    return lax.all_to_all(x, AXIS, split_axis=0, concat_axis=0, tiled=True)


def nt_dot(a, b):
    return lax.dot_general(a, b, (((1,), (1,)), ((), ())), preferred_element_type=F32)


def z_order(planes):
    order = [0]
    bit = planes // 2
    while bit >= 1:
        order = order + [k | bit for k in order]
        bit //= 2
    return order


def row_offsets(n):
    return [(4 * k + 2 * y, c) for y in (0, 1) for k in z_order(n // 4) for c in (0, 1)]


def chip_rows(rows, core, also):
    half = rows.shape[1] // 2
    mine = pick(core, rows[:, :half], rows[:, half:])
    theirs = pick(core, rows[:, half:], rows[:, :half])
    other = after(swap(theirs, 1), *also)
    return pick(core, jnp.concatenate([mine, other]), jnp.concatenate([other, mine]))


def group_rows(blocks, planes):
    column = same(jnp.concatenate([blocks[k] for k in z_order(planes)]))
    both = jnp.concatenate([column, swap(column, 2)])
    return both, swap(both, 1)


def plain_hidden(core, own, other, gate_weight, up_weight):
    both = pick(core, jnp.concatenate([own, other], 1), jnp.concatenate([other, own], 1))
    gate = jnp.dot(both, gate_weight, preferred_element_type=F32)
    up = jnp.dot(both, up_weight, preferred_element_type=F32)
    hidden = jax.nn.silu(gate) * up
    head = lax.reduce_precision(hidden, exponent_bits=8, mantissa_bits=7)
    return head.astype(BF16), (hidden - head).astype(BF16)


class Layout:
    def __init__(self, n, cols, depth, rows, rank):
        self.n, self.cols, self.depth, self.rows, self.rank = n, cols, depth, rows, rank
        self.part = cols // LANES // 3 * LANES
        self.common = cols - 2 * self.part
        self.left = depth // 2
        self.wide = n * rank

    def fits(self, groups):
        return (
            groups % 2 == 0
            and self.cols % LANES == 0
            and self.part > 0
            and self.depth % (2 * LANES) == 0
            and self.depth // LANES * PAD <= self.rank
            and self.rows <= PAD
            and self.n % 16 == 0
        )


def fetch(pairs, sems):
    copies = [pltpu.make_async_copy(source, to, sems.at[at]) for at, (source, to) in enumerate(pairs)]
    for copy in copies:
        copy.start()
    for copy in copies:
        copy.wait()


def split_kernel(lay, plane_ref, right_hbm, left_hbm, split_ref, right_ref, left_ref, sems):
    fetch(((right_hbm, right_ref), (left_hbm, left_ref)), sems)
    plane = plane_ref[0]
    for to in range(lay.n):
        at = pl.multiple_of(to * lay.cols + plane * lay.part, LANES)
        split_ref[to, :, : lay.part] = right_ref[:, pl.ds(at, lay.part)]
        at = pl.multiple_of(to * lay.depth + plane * lay.left, LANES)
        split_ref[to, :, lay.part :] = left_ref[:, pl.ds(at, lay.left)]


def rest_kernel(lay, right_hbm, grad_hbm, rest_ref, right_ref, grad_ref, sems):
    fetch(((right_hbm, right_ref), (grad_hbm, grad_ref)), sems)
    cols, depth, common = lay.cols, lay.depth, lay.common
    for to in range(lay.n):
        rest_ref[to, :, :common] = right_ref[:, to * cols + 2 * lay.part : (to + 1) * cols]
        grad = grad_ref[:, to * depth : (to + 1) * depth].astype(F32)
        grad = jnp.concatenate([grad, jnp.zeros((PAD - lay.rows, depth), F32)]).astype(BF16)
        for piece in range(depth // LANES):
            rest_ref[to, piece * PAD : (piece + 1) * PAD, common:] = grad[:, piece * LANES : (piece + 1) * LANES]


def pack(kernel, name, lay, lanes, scalars, arrays):
    away = pl.BlockSpec(memory_space=pl.ANY)
    return pl.pallas_call(
        functools.partial(kernel, lay),
        in_specs=[pl.BlockSpec(memory_space=pltpu.SMEM)] * len(scalars) + [away] * len(arrays),
        out_specs=pl.BlockSpec(memory_space=pltpu.VMEM),
        out_shape=jax.ShapeDtypeStruct((lay.n, lay.rank, lanes), BF16),
        scratch_shapes=[pltpu.VMEM(x.shape, BF16) for x in arrays] + [pltpu.SemaphoreType.DMA((len(arrays),))],
        compiler_params=pltpu.CompilerParams(vmem_limit_bytes=56 * 2**20),
        cost_estimate=pl.CostEstimate(flops=1000, bytes_accessed=1000, transcendentals=0),
        name=name,
    )(*scalars, *arrays)


def same_kernel(x_ref, out_ref):
    out_ref[...] = x_ref[...]


def same(x):
    whole = pl.BlockSpec(memory_space=pltpu.VMEM)
    return pl.pallas_call(
        same_kernel,
        in_specs=[whole],
        out_specs=whole,
        out_shape=jax.ShapeDtypeStruct(x.shape, x.dtype),
        compiler_params=pltpu.CompilerParams(vmem_limit_bytes=4 * 2**20),
        cost_estimate=pl.CostEstimate(flops=10_000_000_000, bytes_accessed=1000, transcendentals=0),
        name="same",
    )(x)


def hidden_kernel(steps, core_ref, own_ref, other_ref, gate_ref, up_ref, high_ref, low_ref, gate, up):
    step = pl.program_id(0)

    @pl.when(step == 0)
    def _():
        gate[...] = jnp.zeros_like(gate)
        up[...] = jnp.zeros_like(up)

    def add(rows_ref):
        rows = rows_ref[...]
        gate[...] += jnp.dot(rows, gate_ref[...], preferred_element_type=F32)
        up[...] += jnp.dot(rows, up_ref[...], preferred_element_type=F32)

    pl.when(step < steps)(lambda: add(own_ref))
    pl.when(step >= steps)(lambda: add(other_ref))

    @pl.when(step == 2 * steps - 1)
    def _():
        value = gate[...]
        hidden = value / (1.0 + jnp.exp(-value)) * up[...]
        high = hidden.astype(BF16)
        high_ref[...] = high
        low_ref[...] = (hidden - high.astype(F32)).astype(BF16)


def hidden_parts(core, own, other, gate_weight, up_weight):
    rows, half = own.shape
    cols = gate_weight.shape[1]
    steps = max(1, half // 1024)
    step_rows = half // steps
    weight = pl.BlockSpec((step_rows, cols), lambda s, core_ref: ((core_ref[0] * steps + s) % (2 * steps), 0))
    out = pl.BlockSpec((rows, cols), lambda s, core_ref: (0, 0))
    return pl.pallas_call(
        functools.partial(hidden_kernel, steps),
        grid_spec=pltpu.PrefetchScalarGridSpec(
            num_scalar_prefetch=1,
            grid=(2 * steps,),
            in_specs=[
                pl.BlockSpec((rows, step_rows), lambda s, core_ref: (0, jnp.minimum(s, steps - 1))),
                pl.BlockSpec((rows, step_rows), lambda s, core_ref: (0, jnp.maximum(s - steps, 0))),
                weight,
                weight,
            ],
            out_specs=[out, out],
            scratch_shapes=[pltpu.VMEM((rows, cols), F32)] * 2,
        ),
        out_shape=[jax.ShapeDtypeStruct((rows, cols), BF16)] * 2,
        compiler_params=pltpu.CompilerParams(vmem_limit_bytes=48 * 2**20),
        cost_estimate=pl.CostEstimate(flops=1000, bytes_accessed=1000, transcendentals=0),
        name="hidden",
    )(core.reshape(1), own, other, gate_weight, up_weight)


def term_kernel(lay, at_ref, high_ref, low_ref, split_ref, twin_ref, rest_ref, *more):
    keep_ref, send_ref, keep_left_ref, send_left_ref, right, left, grad = more
    here, plane = at_ref[0], at_ref[1]
    core = here & 1
    n, part, common, rank, rows, wide = lay.n, lay.part, lay.common, lay.rank, lay.rows, lay.wide
    for at, (offset, c) in enumerate(row_offsets(n)):
        source = ((here - core) ^ offset) + c
        for piece in range(lay.depth // LANES):
            grad[at * PAD : (at + 1) * PAD, piece * LANES : (piece + 1) * LANES] = rest_ref[
                source, piece * PAD : (piece + 1) * PAD, common:
            ]
    for turn in (0, 1):
        for at in range(n // 2):
            query = turn * (n // 2) + at
            block = slice(query * rank, (query + 1) * rank)
            for side in (0, 1):
                half = jnp.where(plane == side, split_ref[query], twin_ref[query])
                right[block, side * part : (side + 1) * part] = half[:, :part]
                left[block, side * lay.left : (side + 1) * lay.left] = half[:, part:]
            right[block, 2 * part :] = rest_ref[query, :, :common]
        block = slice(turn * wide // 2, (turn + 1) * wide // 2)
        rights = nt_dot(high_ref[...], right[block]) + nt_dot(low_ref[...], right[block])
        lefts = nt_dot(grad[...], left[block])
        for pair in range(n // 2):
            to = slice(pair * rows, (pair + 1) * rows)
            first, second = rights[2 * pair * rows :][:rows], rights[(2 * pair + 1) * rows :][:rows]
            keep_ref[to, block] = jnp.where(core == 0, first, second)
            send_ref[to, block] = jnp.where(core == 0, second, first)
            quarter = n // 8
            at = (pair // quarter & 1) * 2 * quarter + (pair // quarter >> 1) * quarter + pair % quarter
            to = slice(at * rows, (at + 1) * rows)
            first, second = lefts[2 * pair * PAD :][:rows], lefts[(2 * pair + 1) * PAD :][:rows]
            keep_left_ref[to, block] = jnp.where(core == 0, first, second)
            send_left_ref[to, block] = jnp.where(core == 0, second, first)


def terms(lay, here, plane, high, low, split, twin, rest):
    whole = pl.BlockSpec(memory_space=pltpu.VMEM)
    return pl.pallas_call(
        functools.partial(term_kernel, lay),
        in_specs=[pl.BlockSpec(memory_space=pltpu.SMEM)] + [whole] * 5,
        out_specs=[whole] * 4,
        out_shape=[jax.ShapeDtypeStruct((lay.n // 2 * lay.rows, lay.wide), F32)] * 4,
        scratch_shapes=[
            pltpu.VMEM((lay.wide, lay.cols), BF16),
            pltpu.VMEM((lay.wide, lay.depth), BF16),
            pltpu.VMEM((lay.n * PAD, lay.depth), BF16),
        ],
        compiler_params=pltpu.CompilerParams(vmem_limit_bytes=24 * 2**20),
        name="terms",
    )(jnp.stack([here, plane]), high, low, split, twin, rest)


def plain_terms(here, high, low, right, left, grads):
    n, rank = right.shape[:2]
    rows = grads.shape[1]
    core = here & 1
    sources = [((here - core) ^ offset) + c for offset, c in row_offsets(n)]
    grads = jnp.concatenate([lax.dynamic_index_in_dim(grads, source, keepdims=False) for source in sources])
    right, left = right.reshape(n * rank, -1), left.reshape(n * rank, -1)
    both = jnp.concatenate([nt_dot(high, right) + nt_dot(low, right), nt_dot(grads, left)], 1)
    both = both.reshape(n // 2, 2, rows, -1)
    outs = pick(core, both[:, 0], both[:, 1]), pick(core, both[:, 1], both[:, 0])
    return [out.reshape(n // 2 * rows, -1) for out in outs]


def spread(wide, n):
    query = lax.broadcasted_iota(jnp.int32, (wide, n), 0) // (wide // n)
    return (query == lax.broadcasted_iota(jnp.int32, (wide, n), 1)).astype(F32)


def score_kernel(n, right_ref, left_ref, other_ref, out_ref):
    rows, wide = other_ref.shape[0], right_ref.shape[1]
    products = (right_ref[:rows] + other_ref[:, :wide]) * (left_ref[:rows] + other_ref[:, wide:])
    out_ref[...] = jnp.dot(
        products, spread(wide, n), precision=lax.Precision.HIGHEST, preferred_element_type=F32
    )


def score(n, right, left, other):
    whole = pl.BlockSpec(memory_space=pltpu.VMEM)
    return pl.pallas_call(
        functools.partial(score_kernel, n),
        in_specs=[whole] * 3,
        out_specs=whole,
        out_shape=jax.ShapeDtypeStruct((other.shape[0], n), F32),
        compiler_params=pltpu.CompilerParams(vmem_limit_bytes=8 * 2**20),
        name="score",
    )(right, left, other)


def halve(sums, bit):
    half = sums.shape[0] // 2
    return sums[:half] + swap(sums[half:], bit)


def body(tokens, grad_out, gate_weight, up_weight, query_left, query_right):
    n = lax.axis_size(AXIS)
    planes = n // 4
    here = lax.axis_index(AXIS)
    core = here & 1
    own, width = tokens.shape
    rank = query_right.shape[2]
    cols = gate_weight.shape[1]
    depth = width // n
    right_own, left_own = query_right[0].T, query_left[0].T
    lay = Layout(n, cols, width // n, own, rank)
    fits = lay.fits(lax.axis_size("groups"))

    plane = lax.axis_index("groups") & 1
    also = ()
    if fits:
        split = pack(split_kernel, "split", lay, lay.part + lay.left, (plane.reshape(1),), (right_own, left_own))
        also = (split,)
    chip = chip_rows(tokens, core, also)
    blocks = {0: chip}
    for k in range(1, planes):
        blocks[k] = swap(chip, 4 * k)

    if fits:
        split = trade(after(split, chip))
        late = after(grad_out, *blocks.values())
        rest = trade(pack(rest_kernel, "rest", lay, lay.common + LANES, (), (right_own, late)))
        groups = lax.axis_size("groups")
        twin = lax.ppermute(split, "groups", [(g, g ^ 1) for g in range(groups)])
    else:
        cut = lambda x: x.reshape(x.shape[0], n, -1).transpose(1, 0, 2)
        right_all, left_all, grad_all = (trade(cut(x)) for x in (right_own, left_own, grad_out))

    own_half, other_half = group_rows(blocks, planes)
    if fits:
        high, low = hidden_parts(core, own_half, other_half, gate_weight, up_weight)
        keep, send, keep_left, send_left = terms(lay, here, plane, high, low, split, twin, rest)
        right, left = keep + swap(send, 1), keep_left + swap(send_left, 1)
        right, left = halve(right, 2), halve(left, 4)
        right, left = halve(right, 4), halve(left, 2)
        bit = 8
        while 2 * bit < n:
            right, left = halve(right, bit), halve(left, bit)
            bit *= 2
        other = swap(jnp.concatenate([right[own:], left[own:]], 1), bit)
        return score(n, right, left, other)

    high, low = plain_hidden(core, own_half, other_half, gate_weight, up_weight)
    keep, send = plain_terms(here, high, low, right_all, left_all, grad_all)

    sums = keep + swap(send, 1)
    bit = 2
    while bit < n:
        sums = halve(sums, bit)
        bit *= 2
    wide = n * rank
    return jnp.dot(sums[:, :wide] * sums[:, wide:], spread(wide, n), precision=lax.Precision.HIGHEST)


def solution(mesh):
    return jax.shard_map(
        body,
        mesh=mesh,
        in_specs=(
            P(("groups", "query"), None),
            P(("groups", "query"), None),
            P(None, "query"),
            P(None, "query"),
            P("query", None, None),
            P("query", None, None),
        ),
        out_specs=P(("groups", "query"), None),
        check_vma=False,
    )
```
